512 devices in a mesh: views: 32 (over x, z), heads: 16 (over y, core).
Axes of the slice: x: 4, y: 8, z: 8, core: 2. Of those that a mesh axis runs over, the one named last changes fastest.
Arguments:
- queries: bfloat16 [8192, 1024], P('views', 'heads'), may hold values from -12 to 12
- keys: bfloat16 [65536, 1024], P('views', 'heads'), may hold values from -6 to 6
- values: bfloat16 [65536, 1024], P('views', 'heads'), may hold values from -6 to 6
- out_weight: bfloat16 [1024, 1024], replicated, may hold values from -0.1875 to 0.1875
Outputs:
- attended: bfloat16 [8192, 1024], P(('views', 'heads'))
The draws below stay inside these ranges and needn't reach their ends.
All inputs are finite; a program needn't handle non-finite values.
Results may differ from the reference program's by a relative error of at most 0.01265.
Values may be sent and summed in bfloat16 or wider, within the bound.
No kernel may reach another device: no remote copies, remote signals or barrier semaphores. Data moves between devices by JAX's collectives and lax.ppermute only.
A program may use at most 64 MiB of HBM per device.

```python
import jax
import jax.numpy as jnp
from jax import lax

HEADS = 16
HEAD_DIM = 64
D = 1024
QROWS = 8192
KV = 65536


def loose_table():
    return jnp.array([8.0, 9.0, 10.0, 12.0], jnp.float32)


def draw_queries(key, part):
    key = jax.random.fold_in(key, 11)
    loose_flips = jax.random.bernoulli(jax.random.fold_in(key, 5), 0.5, (4, D)).astype(jnp.float32)
    loose_signs = 2.0 * loose_flips - 1.0
    loose_places = jnp.arange(4, dtype=jnp.int32) * (QROWS // 4) + QROWS // 8 + 5
    drawn = jnp.clip(jax.random.normal(key, (QROWS, D), jnp.float32), -4.0, 4.0)
    drawn = drawn.at[loose_places].set(loose_table()[:, None] * loose_signs)
    return drawn.astype(jnp.bfloat16)


def draw_keys(key, part):
    key = jax.random.fold_in(key, 23)
    drawn = jnp.clip(jax.random.normal(key, (KV, D), jnp.float32), -4.0, 4.0)
    return drawn.astype(jnp.bfloat16)


def shard_levels(stream_key, extent, split, low, high):
    gain, own = 1.0, jax.random.fold_in(stream_key, 6)
    for axis_at, blocks in split:
        steps = jnp.exp(jax.random.uniform(jax.random.fold_in(own, axis_at), (blocks,), jnp.float32, low / len(split), high / len(split)))
        gain = gain * jnp.repeat(steps, extent[axis_at] // blocks).reshape([-1 if axis == axis_at else 1 for axis in range(len(extent))])
    return gain


def noise(stream_key, shape, scale, reach, split=(), kind=jnp.bfloat16):
    gain = shard_levels(stream_key, shape, split, -0.22, 0.18) if split else 1.0
    result = jax.random.normal(stream_key, shape, jnp.float32) * scale * gain
    return jnp.minimum(jnp.maximum(result, -reach), reach).astype(kind)


def setup_inputs(seed: int = 0) -> dict:
    key_of = jax.random.split(jax.random.key(seed), 5)
    return {
        "queries": draw_queries(jax.random.fold_in(key_of[4], 71), 0),
        "keys": draw_keys(jax.random.fold_in(key_of[4], 71), 0),
        "values": noise(key_of[2], (KV, D), 1.0, 6.0, ((0, 32), (1, 16))),
        "out_weight": noise(key_of[3], (D, D), D ** -0.5, 0.1875),
    }


def reference(queries, keys, values, out_weight):
    rows = queries.shape[0]
    block = 512 if rows % 512 == 0 else rows
    scale = HEAD_DIM ** -0.5
    query_heads = queries.reshape(rows // block, block, HEADS, HEAD_DIM).transpose(2, 0, 1, 3)
    key_heads = keys.reshape(-1, HEADS, HEAD_DIM).transpose(1, 0, 2)
    value_heads = values.reshape(-1, HEADS, HEAD_DIM).transpose(1, 0, 2)

    def one_head(packed):
        query_blocks, key_rows, value_rows = packed

        def one_block(query_block):
            scores = jnp.dot(query_block, key_rows.T, preferred_element_type=jnp.float32) * scale
            peak = jnp.max(scores, axis=1)
            weights = jnp.exp(scores - peak[:, None])
            total = jnp.sum(weights, axis=1)
            summed = jnp.dot(weights.astype(jnp.bfloat16), value_rows, preferred_element_type=jnp.float32)
            return (summed / total[:, None]).astype(jnp.bfloat16)

        return lax.map(one_block, query_blocks)

    heads_out = lax.map(one_head, (query_heads, key_heads, value_heads))
    heads_out = heads_out.transpose(1, 2, 0, 3).reshape(rows, HEADS * HEAD_DIM)
    return jnp.dot(heads_out, out_weight, preferred_element_type=jnp.float32).astype(jnp.bfloat16)
```

```python
import functools

import jax
import jax.numpy as jnp
from jax import lax
from jax.experimental import pallas as pl
from jax.experimental.pallas import tpu as pltpu
from jax.sharding import PartitionSpec as P

HEAD_DIM = 64
LOG2E = 1.4426950408889634
X, Z = 4, 8
ONES = 16
PART = 512
WIDE = 128
LIMIT = 2.0**100
VMEM = 48 * 2**20


def _dot(a, b, ca, cb):
    return lax.dot_general(a, b, (((ca,), (cb,)), ((), ())), preferred_element_type=jnp.float32)


def _attend_kernel(chunks, first, last, *refs):
    q_ref, kv_refs = refs[0], refs[1 : 1 + chunks]
    state_ref = None if first else refs[1 + chunks]
    if last:
        out_ref, hold_ref = refs[-2:]
    else:
        out_ref = hold_ref = refs[-1]
    blocks, _, block = q_ref.shape
    rows = blocks * block
    keys = kv_refs[0].shape[1]
    scale = HEAD_DIM ** (-0.5) * LOG2E
    ones = jnp.ones((ONES, PART), jnp.bfloat16)

    def queries():
        return jnp.concatenate([q_ref[b] for b in range(blocks)], axis=1)

    def score(kv_ref, at, q):
        return _dot(kv_ref[0:HEAD_DIM, pl.ds(at, PART)], q, 0, 0) * scale

    def weigh(kv_ref, at, weights):
        v = jnp.concatenate([kv_ref[HEAD_DIM : 2 * HEAD_DIM, pl.ds(at, PART)], ones], axis=0)
        return _dot(v, weights.astype(jnp.bfloat16), 1, 0)

    q = queries()
    total = jnp.zeros((HEAD_DIM + ONES, rows), jnp.float32) if first else state_ref[...]
    peak = None if first else state_ref[72:73, :]
    for kv_ref in kv_refs:
        for at in range(0, keys, PART):
            s = score(kv_ref, at, q)
            if peak is None:
                peak = jnp.max(s, axis=0, keepdims=True)
            total = total + weigh(kv_ref, at, jnp.exp2(s - peak))
    hold_ref[0:72, :] = total[0:72]
    hold_ref[72:80, :] = jnp.broadcast_to(peak, (8, rows))
    in_range = jnp.max(total[64:65]) < LIMIT

    @pl.when(jnp.logical_not(in_range))
    def _():
        q = queries()
        if first:
            hold_ref[0:72, :] = jnp.zeros((72, rows), jnp.float32)
            hold_ref[72:80, :] = jnp.full((8, rows), -1e30, jnp.float32)
        else:
            hold_ref[...] = state_ref[...]
        for kv_ref in kv_refs:

            @pl.loop(0, keys // PART)
            def _(i):
                at = pl.multiple_of(i * PART, PART)
                s = score(kv_ref, at, q)
                old = hold_ref[72:73, :]
                new = jnp.maximum(old, jnp.max(s, axis=0, keepdims=True))
                more = weigh(kv_ref, at, jnp.exp2(s - new))
                hold_ref[0:72, :] = hold_ref[0:72, :] * jnp.exp2(old - new) + more[0:72]
                hold_ref[72:80, :] = jnp.broadcast_to(new, (8, rows))

    if last:
        def head(x):
            return x.astype(jnp.bfloat16).astype(jnp.float32)

        t = hold_ref[64:72, :]
        p = hold_ref[72:80, :]
        t0 = head(t)
        p0 = head(p)
        p1 = head(p - p0)
        p2 = p - p0 - p1
        at = lax.broadcasted_iota(jnp.int32, (8, rows), 0)
        tail = jnp.where(at == 0, t0, 0.0)
        for i, x in ((1, t - t0), (2, p0), (3, p1), (4, p2)):
            tail = jnp.where(at == i, x, tail)
        both = jnp.concatenate(
            [hold_ref[0:HEAD_DIM, :], tail, jnp.zeros((WIDE - HEAD_DIM - 8, rows), jnp.float32)], axis=0
        )
        out_ref[...] = both.T.astype(jnp.bfloat16)


def _attend(q_all, kvs, state, last):
    blocks, _, block = q_all.shape
    rows = blocks * block
    state_type = jax.ShapeDtypeStruct((80, rows), jnp.float32)
    operands = (q_all, *kvs) + (() if state is None else (state,))
    keys = len(kvs) * kvs[0].shape[1]
    return pl.pallas_call(
        functools.partial(_attend_kernel, len(kvs), state is None, last),
        out_shape=jax.ShapeDtypeStruct((rows, WIDE), jnp.bfloat16) if last else state_type,
        in_specs=[pl.BlockSpec(memory_space=pltpu.VMEM)] * len(operands),
        out_specs=pl.BlockSpec(memory_space=pltpu.VMEM),
        scratch_shapes=[pltpu.VMEM((80, rows), jnp.float32)] if last else [],
        compiler_params=pltpu.CompilerParams(vmem_limit_bytes=VMEM),
        cost_estimate=pl.CostEstimate(
            flops=4 * rows * keys * 256, bytes_accessed=2**21, transcendentals=rows * keys
        ),
    )(*operands)


def _finish_kernel(own, heads, got_ref, weight_ref, out_ref):
    n = heads * own
    col = lax.broadcasted_iota(jnp.int32, (WIDE, 2 * WIDE), 0)
    half = lax.broadcasted_iota(jnp.int32, (WIDE, 2 * WIDE), 1) // WIDE
    pick = ((half == 0) & (col >= 64) & (col < 66)) | ((half == 1) & (col >= 66) & (col < 69))
    pick = jnp.where(pick, 1.0, 0.0).astype(jnp.bfloat16)
    parts = [got_ref[z * n : (z + 1) * n, :] for z in range(Z)]
    spread = [_dot(part, pick, 1, 0) for part in parts]
    top = spread[0][:, WIDE:]
    for s in spread[1:]:
        top = jnp.maximum(top, s[:, WIDE:])
    summed = jnp.zeros((n, WIDE), jnp.float32)
    total = jnp.zeros((n, WIDE), jnp.float32)
    for part, s in zip(parts, spread):
        factor = jnp.exp2(s[:, WIDE:] - top)
        summed += factor * part.astype(jnp.float32)
        total += factor * s[:, :WIDE]
    out = summed / total
    lane = lax.broadcasted_iota(jnp.int32, (own, WIDE), 1)
    acc = jnp.zeros(out_ref.shape, jnp.float32)
    per = 4
    for g in range(heads // per):
        pairs = []
        for h in range(g * per, (g + 1) * per, 2):
            even = out[h * own : (h + 1) * own]
            odd = pltpu.roll(out[(h + 1) * own : (h + 2) * own], HEAD_DIM, 1)
            pairs.append(jnp.where(lane < HEAD_DIM, even, odd).astype(jnp.bfloat16))
        w = weight_ref[g * per * HEAD_DIM : (g + 1) * per * HEAD_DIM, :]
        acc += _dot(jnp.concatenate(pairs, axis=1), w, 1, 0)
    out_ref[...] = acc.astype(jnp.bfloat16)


def _finish(got, out_weight, own, heads):
    return pl.pallas_call(
        functools.partial(_finish_kernel, own, heads),
        out_shape=jax.ShapeDtypeStruct((own, out_weight.shape[1]), jnp.bfloat16),
        in_specs=[pl.BlockSpec(memory_space=pltpu.VMEM)] * 2,
        out_specs=pl.BlockSpec(memory_space=pltpu.VMEM),
        compiler_params=pltpu.CompilerParams(vmem_limit_bytes=VMEM),
    )(got, out_weight)


def per_device(heads, queries, keys, values, out_weight):
    z_groups = [[x * Z + z for z in range(Z)] for x in range(X)]
    zh_groups = [[(x * Z + z) * heads + h for z in range(Z) for h in range(heads)] for x in range(X)]

    def from_x(array, step):
        return lax.ppermute(
            array, "views", [(x * Z + z, (x + step) % X * Z + z) for x in range(X) for z in range(Z)]
        )

    copies = jnp.broadcast_to(queries.T[None], (Z, HEAD_DIM, queries.shape[0]))
    q_all = lax.all_to_all(copies, "views", 0, 0, tiled=True, axis_index_groups=z_groups)
    kv = jnp.concatenate([keys.T, values.T], axis=0)
    kv1, kv3, kv2 = from_x(kv, 1), from_x(kv, 3), from_x(kv, 2)
    state = _attend(q_all, (kv,), None, False)
    state = _attend(q_all, (kv1, kv3), state, False)
    rows = _attend(q_all, (kv2,), state, True)

    own = queries.shape[0] // heads
    sent = rows.reshape(Z * heads, own, WIDE)
    got = lax.all_to_all(sent, ("views", "heads"), 0, 0, tiled=True, axis_index_groups=zh_groups)
    return _finish(got.reshape(Z * heads * own, WIDE), out_weight, own, heads)


def solution(mesh):
    assert mesh.shape["views"] == X * Z
    return jax.shard_map(
        functools.partial(per_device, mesh.shape["heads"]),
        mesh=mesh,
        in_specs=(P("views", "heads"), P("views", "heads"), P("views", "heads"), P()),
        out_specs=P(("views", "heads"), None),
        check_vma=False,
    )
```

```python
import functools

import jax
import jax.numpy as jnp
from jax import lax
from jax.experimental import pallas as pl
from jax.experimental.pallas import tpu as pltpu
from jax.sharding import PartitionSpec as P

HEAD_DIM = 64
LOG2E = 1.4426950408889634
X, Z = 4, 8
ONES = 16
PART = 512
WIDE = 128
LIMIT = 2.0**100
VMEM = 48 * 2**20


def _dot(a, b, ca, cb):
    return lax.dot_general(a, b, (((ca,), (cb,)), ((), ())), preferred_element_type=jnp.float32)


def _prepare_kernel(q_ref, k_ref, v_ref, copies_ref, kv_ref):
    kv_ref[0:HEAD_DIM, :] = k_ref[...]
    kv_ref[HEAD_DIM : 2 * HEAD_DIM, :] = v_ref[...]
    q = q_ref[...]
    for z in range(Z):
        copies_ref[z] = q


def _prepare(q, k, v):
    return pl.pallas_call(
        _prepare_kernel,
        out_shape=[
            jax.ShapeDtypeStruct((Z, *q.shape), q.dtype),
            jax.ShapeDtypeStruct((2 * HEAD_DIM, k.shape[1]), k.dtype),
        ],
        in_specs=[pl.BlockSpec(memory_space=pltpu.VMEM)] * 3,
        out_specs=[pl.BlockSpec(memory_space=pltpu.VMEM)] * 2,
        compiler_params=pltpu.CompilerParams(vmem_limit_bytes=62 * 2**20),
    )(q, k, v)


def _attend_kernel(chunks, first, last, *refs):
    q_ref, kv_refs = refs[0], refs[1 : 1 + chunks]
    state_ref = None if first else refs[1 + chunks]
    if last:
        out_ref, hold_ref = refs[-2:]
    else:
        out_ref = hold_ref = refs[-1]
    blocks, _, block = q_ref.shape
    rows = blocks * block
    keys = kv_refs[0].shape[1]
    scale = HEAD_DIM ** (-0.5) * LOG2E
    ones = jnp.ones((ONES, PART), jnp.bfloat16)

    def queries():
        return jnp.concatenate([q_ref[b] for b in range(blocks)], axis=1)

    def score(kv_ref, at, q):
        return _dot(kv_ref[0:HEAD_DIM, pl.ds(at, PART)], q, 0, 0) * scale

    def weigh(kv_ref, at, weights):
        v = jnp.concatenate([kv_ref[HEAD_DIM : 2 * HEAD_DIM, pl.ds(at, PART)], ones], axis=0)
        return _dot(v, weights.astype(jnp.bfloat16), 1, 0)

    q = queries()
    total = jnp.zeros((HEAD_DIM + ONES, rows), jnp.float32) if first else state_ref[...]
    peak = None if first else state_ref[72:73, :]
    for kv_ref in kv_refs:
        for at in range(0, keys, PART):
            s = score(kv_ref, at, q)
            if peak is None:
                peak = jnp.max(s, axis=0, keepdims=True)
            total = total + weigh(kv_ref, at, jnp.exp2(s - peak))
    hold_ref[0:72, :] = total[0:72]
    hold_ref[72:80, :] = jnp.broadcast_to(peak, (8, rows))
    in_range = jnp.max(total[64:65]) < LIMIT

    @pl.when(jnp.logical_not(in_range))
    def _():
        q = queries()
        if first:
            hold_ref[0:72, :] = jnp.zeros((72, rows), jnp.float32)
            hold_ref[72:80, :] = jnp.full((8, rows), -1e30, jnp.float32)
        else:
            hold_ref[...] = state_ref[...]
        for kv_ref in kv_refs:

            @pl.loop(0, keys // PART)
            def _(i):
                at = pl.multiple_of(i * PART, PART)
                s = score(kv_ref, at, q)
                old = hold_ref[72:73, :]
                new = jnp.maximum(old, jnp.max(s, axis=0, keepdims=True))
                more = weigh(kv_ref, at, jnp.exp2(s - new))
                hold_ref[0:72, :] = hold_ref[0:72, :] * jnp.exp2(old - new) + more[0:72]
                hold_ref[72:80, :] = jnp.broadcast_to(new, (8, rows))

    if last:
        def head(x):
            return x.astype(jnp.bfloat16).astype(jnp.float32)

        t = hold_ref[64:72, :]
        p = hold_ref[72:80, :]
        t0 = head(t)
        p0 = head(p)
        p1 = head(p - p0)
        p2 = p - p0 - p1
        at = lax.broadcasted_iota(jnp.int32, (8, rows), 0)
        tail = jnp.where(at == 0, t0, 0.0)
        for i, x in ((1, t - t0), (2, p0), (3, p1), (4, p2)):
            tail = jnp.where(at == i, x, tail)
        both = jnp.concatenate(
            [hold_ref[0:HEAD_DIM, :], tail, jnp.zeros((WIDE - HEAD_DIM - 8, rows), jnp.float32)], axis=0
        )
        out_ref[...] = both.T.astype(jnp.bfloat16)


def _attend(q_all, kvs, state, last):
    blocks, _, block = q_all.shape
    rows = blocks * block
    state_type = jax.ShapeDtypeStruct((80, rows), jnp.float32)
    operands = (q_all, *kvs) + (() if state is None else (state,))
    keys = len(kvs) * kvs[0].shape[1]
    return pl.pallas_call(
        functools.partial(_attend_kernel, len(kvs), state is None, last),
        out_shape=jax.ShapeDtypeStruct((rows, WIDE), jnp.bfloat16) if last else state_type,
        in_specs=[pl.BlockSpec(memory_space=pltpu.VMEM)] * len(operands),
        out_specs=pl.BlockSpec(memory_space=pltpu.VMEM),
        scratch_shapes=[pltpu.VMEM((80, rows), jnp.float32)] if last else [],
        compiler_params=pltpu.CompilerParams(vmem_limit_bytes=VMEM),
        cost_estimate=pl.CostEstimate(
            flops=4 * rows * keys * 256, bytes_accessed=2**21, transcendentals=rows * keys
        ),
    )(*operands)


def _finish_kernel(own, heads, got_ref, weight_ref, out_ref):
    n = heads * own
    col = lax.broadcasted_iota(jnp.int32, (WIDE, 2 * WIDE), 0)
    half = lax.broadcasted_iota(jnp.int32, (WIDE, 2 * WIDE), 1) // WIDE
    pick = ((half == 0) & (col >= 64) & (col < 66)) | ((half == 1) & (col >= 66) & (col < 69))
    pick = jnp.where(pick, 1.0, 0.0).astype(jnp.bfloat16)
    parts = [got_ref[i * n : (i + 1) * n, :] for i in range(got_ref.shape[0] // n)]
    spread = [_dot(part, pick, 1, 0) for part in parts]
    top = spread[0][:, WIDE:]
    for s in spread[1:]:
        top = jnp.maximum(top, s[:, WIDE:])
    summed = jnp.zeros((n, WIDE), jnp.float32)
    total = jnp.zeros((n, WIDE), jnp.float32)
    for part, s in zip(parts, spread):
        factor = jnp.exp2(s[:, WIDE:] - top)
        summed += factor * part.astype(jnp.float32)
        total += factor * s[:, :WIDE]
    out = summed / total
    lane = lax.broadcasted_iota(jnp.int32, (own, WIDE), 1)
    acc = jnp.zeros(out_ref.shape, jnp.float32)
    per = 4
    for g in range(heads // per):
        pairs = []
        for h in range(g * per, (g + 1) * per, 2):
            even = out[h * own : (h + 1) * own]
            odd = pltpu.roll(out[(h + 1) * own : (h + 2) * own], HEAD_DIM, 1)
            pairs.append(jnp.where(lane < HEAD_DIM, even, odd).astype(jnp.bfloat16))
        w = weight_ref[g * per * HEAD_DIM : (g + 1) * per * HEAD_DIM, :]
        acc += _dot(jnp.concatenate(pairs, axis=1), w, 1, 0)
    out_ref[...] = acc.astype(jnp.bfloat16)


def _finish(got, out_weight, own, heads):
    return pl.pallas_call(
        functools.partial(_finish_kernel, own, heads),
        out_shape=jax.ShapeDtypeStruct((own, out_weight.shape[1]), jnp.bfloat16),
        in_specs=[pl.BlockSpec(memory_space=pltpu.VMEM)] * 2,
        out_specs=pl.BlockSpec(memory_space=pltpu.VMEM),
        compiler_params=pltpu.CompilerParams(vmem_limit_bytes=VMEM),
    )(got, out_weight)


def per_device(heads, queries, keys, values, out_weight):
    z_groups = [[x * Z + z for z in range(Z)] for x in range(X)]
    zh_groups = [[(x * Z + z) * heads + h for z in range(Z) for h in range(heads)] for x in range(X)]

    def from_x(array, step):
        return lax.ppermute(
            array, "views", [(x * Z + z, (x + step) % X * Z + z) for x in range(X) for z in range(Z)]
        )

    copies, kv = _prepare(queries.T, keys.T, values.T)
    kv2 = from_x(kv, 2)
    q_all = lax.all_to_all(copies, "views", 0, 0, tiled=True, axis_index_groups=z_groups)
    kv1, kv3 = from_x(kv, 1), from_x(kv, 3)
    state = _attend(q_all, (kv, kv2), None, False)
    state = _attend(q_all, (kv1,), state, False)
    rows = _attend(q_all, (kv3,), state, True)

    own = queries.shape[0] // heads
    sent = rows.reshape(Z * heads, own, WIDE)
    got = lax.all_to_all(sent, ("views", "heads"), 0, 0, tiled=True, axis_index_groups=zh_groups)
    return _finish(got.reshape(Z * heads * own, WIDE), out_weight, own, heads)


def solution(mesh):
    assert mesh.shape["views"] == X * Z
    return jax.shard_map(
        functools.partial(per_device, mesh.shape["heads"]),
        mesh=mesh,
        in_specs=(P("views", "heads"), P("views", "heads"), P("views", "heads"), P()),
        out_specs=P(("views", "heads"), None),
        check_vma=False,
    )
```

```python
import functools

import jax
import jax.numpy as jnp
from jax import lax
from jax.experimental import pallas as pl
from jax.experimental.pallas import tpu as pltpu
from jax.sharding import PartitionSpec as P

HEAD_DIM = 64
LOG2E = 1.4426950408889634
X, Z = 4, 8
ONES = 16
PART = 512
WIDE = 128
OWN = 16
SENT = 10
LIMIT = 2.0**100
VMEM = 48 * 2**20


def _dot(a, b, ca, cb):
    return lax.dot_general(a, b, (((ca,), (cb,)), ((), ())), preferred_element_type=jnp.float32)


def _copies_kernel(q_ref, copies_ref):
    n = q_ref.shape[1]
    row = lax.broadcasted_iota(jnp.int32, (n, n), 0)
    to = lax.broadcasted_iota(jnp.int32, (n, n), 1)
    move = row // OWN * 8 + row % 8 + row % OWN // 8 * (n // 2) == to
    q = _dot(q_ref[...], jnp.where(move, 1.0, 0.0).astype(jnp.bfloat16), 1, 0).astype(jnp.bfloat16)
    for z in range(copies_ref.shape[0]):
        copies_ref[z] = q


def _copies(q):
    return pl.pallas_call(
        _copies_kernel,
        out_shape=jax.ShapeDtypeStruct((Z, *q.shape), q.dtype),
        in_specs=[pl.BlockSpec(memory_space=pltpu.VMEM)],
        out_specs=pl.BlockSpec(memory_space=pltpu.VMEM),
        compiler_params=pltpu.CompilerParams(vmem_limit_bytes=62 * 2**20),
    )(q)


def _attend_kernel(chunks, first, last, *refs):
    q_ref, kv_refs = refs[0], refs[1 : 1 + chunks]
    state_ref = None if first else refs[1 + chunks]
    if last:
        out_ref, hold_ref, pack_ref = refs[-3:]
    else:
        out_ref = hold_ref = refs[-1]
    blocks, _, block = q_ref.shape
    rows = blocks * block
    keys = kv_refs[0].shape[1]
    scale = HEAD_DIM ** (-0.5) * LOG2E
    ones = jnp.ones((ONES, PART), jnp.bfloat16)

    def queries():
        parts = [q_ref[b, :, u * block // 2 : (u + 1) * block // 2] for u in range(2) for b in range(blocks)]
        return jnp.concatenate(parts, axis=1)

    def score(kv_ref, at, q):
        return _dot(kv_ref[0:HEAD_DIM, pl.ds(at, PART)], q, 0, 0) * scale

    def weigh(kv_ref, at, weights):
        v = jnp.concatenate([kv_ref[HEAD_DIM : 2 * HEAD_DIM, pl.ds(at, PART)], ones], axis=0)
        return _dot(v, weights.astype(jnp.bfloat16), 1, 0)

    q = queries()
    total = jnp.zeros((HEAD_DIM + ONES, rows), jnp.float32) if first else state_ref[...]
    peak = None if first else state_ref[72:73, :]
    for kv_ref in kv_refs:
        for at in range(0, keys, PART):
            s = score(kv_ref, at, q)
            if peak is None:
                peak = jnp.max(s, axis=0, keepdims=True)
            total = total + weigh(kv_ref, at, jnp.exp2(s - peak))
    hold_ref[0:72, :] = total[0:72]
    hold_ref[72:80, :] = jnp.broadcast_to(peak, (8, rows))
    in_range = jnp.max(total[64:65]) < LIMIT

    @pl.when(jnp.logical_not(in_range))
    def _():
        q = queries()
        if first:
            hold_ref[0:72, :] = jnp.zeros((72, rows), jnp.float32)
            hold_ref[72:80, :] = jnp.full((8, rows), -1e30, jnp.float32)
        else:
            hold_ref[...] = state_ref[...]
        for kv_ref in kv_refs:

            @pl.loop(0, keys // PART)
            def _(i):
                at = pl.multiple_of(i * PART, PART)
                s = score(kv_ref, at, q)
                old = hold_ref[72:73, :]
                new = jnp.maximum(old, jnp.max(s, axis=0, keepdims=True))
                more = weigh(kv_ref, at, jnp.exp2(s - new))
                hold_ref[0:72, :] = hold_ref[0:72, :] * jnp.exp2(old - new) + more[0:72]
                hold_ref[72:80, :] = jnp.broadcast_to(new, (8, rows))

    if last:
        def head(x):
            return x.astype(jnp.bfloat16).astype(jnp.float32)

        half = rows // 2
        count = half // 8
        both = jnp.concatenate([hold_ref[0:HEAD_DIM, :half], hold_ref[0:HEAD_DIM, half:]], axis=0).T
        t = hold_ref[64:72, :]
        p = hold_ref[72:80, :]
        t0 = head(t)
        p0 = head(p)
        p1 = head(p - p0)
        terms = (t0, t - t0, p0, p1, p - p0 - p1)
        owner = lax.broadcasted_iota(jnp.int32, (8, WIDE), 0)
        lane = lax.broadcasted_iota(jnp.int32, (8, WIDE), 1)
        mine = []
        for c in range(0, count, 8):
            at = c * 8 // WIDE * WIDE
            here = lane // 8 == owner + c % (WIDE // 8)
            cols = [jnp.where(here, x[:, u * half + at : u * half + at + WIDE], 0.0) for x in terms for u in range(2)]
            mine.append(jnp.concatenate(cols, axis=1).astype(jnp.bfloat16))
        source = lax.broadcasted_iota(jnp.int32, (10 * WIDE, WIDE), 0)
        to = lax.broadcasted_iota(jnp.int32, (10 * WIDE, WIDE), 1)
        move = jnp.where(source // WIDE * 8 + source % 8 == to, 1.0, 0.0).astype(jnp.bfloat16)
        tail = _dot(jnp.concatenate(mine, axis=0), move, 1, 0)
        for c in range(count):
            pack_ref[c * SENT : c * SENT + 8, :] = both[c * 8 : c * 8 + 8]
            pack_ref[c * SENT + 8 : c * SENT + 10, :] = jnp.broadcast_to(tail[c : c + 1], (2, WIDE))
        out_ref[...] = pack_ref[...].astype(jnp.bfloat16)


def _attend(q_all, kvs, state, last):
    blocks, _, block = q_all.shape
    rows = blocks * block
    state_type = jax.ShapeDtypeStruct((80, rows), jnp.float32)
    operands = (q_all, *kvs) + (() if state is None else (state,))
    keys = len(kvs) * kvs[0].shape[1]
    return pl.pallas_call(
        functools.partial(_attend_kernel, len(kvs), state is None, last),
        out_shape=jax.ShapeDtypeStruct((rows // OWN * SENT, WIDE), jnp.bfloat16) if last else state_type,
        in_specs=[pl.BlockSpec(memory_space=pltpu.VMEM)] * len(operands),
        out_specs=pl.BlockSpec(memory_space=pltpu.VMEM),
        scratch_shapes=[pltpu.VMEM((80, rows), jnp.float32), pltpu.VMEM((rows // OWN * SENT, WIDE), jnp.float32)]
        if last
        else [],
        compiler_params=pltpu.CompilerParams(vmem_limit_bytes=VMEM),
        cost_estimate=pl.CostEstimate(
            flops=4 * rows * keys * 256, bytes_accessed=2**21, transcendentals=rows * keys
        ),
    )(*operands)


def _finish_kernel(heads, got_ref, weight_ref, out_ref, pack_ref):
    senders = got_ref.shape[0] // (heads * SENT)
    pack_ref[...] = got_ref[...].astype(jnp.float32)
    lane = lax.broadcasted_iota(jnp.int32, (8, WIDE), 1)
    sub = lax.broadcasted_iota(jnp.int32, (8, WIDE), 0)
    mine = (lane % 8 == sub) & (lane < 5 * OWN)
    term = lax.broadcasted_iota(jnp.int32, (WIDE, 2 * WIDE), 0)
    to = lax.broadcasted_iota(jnp.int32, (WIDE, 2 * WIDE), 1)
    pick = ((term // OWN < 2) == (to < WIDE)) & ((term % OWN < 8) == (to % WIDE < HEAD_DIM))
    pick = jnp.where(pick, 1.0, 0.0).astype(jnp.bfloat16)
    parts, spread = [], []
    for s in range(senders):
        at = [(s * heads + h) * SENT for h in range(heads)]
        parts.append(jnp.concatenate([pack_ref[i : i + 8, :] for i in at], axis=0))
        tails = [jnp.where(mine, jnp.broadcast_to(pack_ref[i + 8 : i + 9, :], (8, WIDE)), 0.0) for i in at]
        spread.append(_dot(jnp.concatenate(tails, axis=0).astype(jnp.bfloat16), pick, 1, 0))
    top = spread[0][:, WIDE:]
    for s in spread[1:]:
        top = jnp.maximum(top, s[:, WIDE:])
    summed = jnp.zeros((8 * heads, WIDE), jnp.float32)
    total = jnp.zeros((8 * heads, WIDE), jnp.float32)
    for part, s in zip(parts, spread):
        factor = jnp.exp2(s[:, WIDE:] - top)
        summed += factor * part
        total += factor * s[:, :WIDE]
    out = summed / total
    acc = jnp.zeros(out_ref.shape, jnp.float32)
    per = 4
    for g in range(heads // per):
        pairs = []
        for h in range(g * per, (g + 1) * per, 2):
            even = out[h * 8 : (h + 1) * 8]
            odd = out[(h + 1) * 8 : (h + 2) * 8]
            low = jnp.where(lane < HEAD_DIM, even, pltpu.roll(odd, HEAD_DIM, 1))
            high = jnp.where(lane < HEAD_DIM, pltpu.roll(even, HEAD_DIM, 1), odd)
            pairs.append(jnp.concatenate([low, high], axis=0).astype(jnp.bfloat16))
        w = weight_ref[g * per * HEAD_DIM : (g + 1) * per * HEAD_DIM, :]
        acc += _dot(jnp.concatenate(pairs, axis=1), w, 1, 0)
    out_ref[...] = acc.astype(jnp.bfloat16)


def _finish(got, out_weight, heads):
    return pl.pallas_call(
        functools.partial(_finish_kernel, heads),
        out_shape=jax.ShapeDtypeStruct((OWN, out_weight.shape[1]), jnp.bfloat16),
        in_specs=[pl.BlockSpec(memory_space=pltpu.VMEM)] * 2,
        out_specs=pl.BlockSpec(memory_space=pltpu.VMEM),
        scratch_shapes=[pltpu.VMEM(got.shape, jnp.float32)],
        compiler_params=pltpu.CompilerParams(vmem_limit_bytes=VMEM),
    )(got, out_weight)


def per_device(heads, queries, keys, values, out_weight):
    z_groups = [[x * Z + z for z in range(Z)] for x in range(X)]
    zh_groups = [[(x * Z + z) * heads + h for z in range(Z) for h in range(heads)] for x in range(X)]

    def from_x(array, step):
        return lax.ppermute(
            array, "views", [(x * Z + z, (x + step) % X * Z + z) for x in range(X) for z in range(Z)]
        )

    kv = jnp.concatenate([keys.T, values.T], axis=0)
    kv2 = from_x(kv, 2)
    q_all = lax.all_to_all(_copies(queries.T), "views", 0, 0, tiled=True, axis_index_groups=z_groups)
    kv1, kv3 = from_x(kv, 1), from_x(kv, 3)
    state = _attend(q_all, (kv, kv2), None, False)
    state = _attend(q_all, (kv1,), state, False)
    rows = _attend(q_all, (kv3,), state, True)

    sent = rows.reshape(Z * heads * SENT // 2, 2, WIDE)
    got = lax.all_to_all(sent, ("views", "heads"), 0, 0, tiled=True, axis_index_groups=zh_groups)
    return _finish(got.reshape(Z * heads * SENT, WIDE), out_weight, heads)


def solution(mesh):
    assert mesh.shape["views"] == X * Z
    return jax.shard_map(
        functools.partial(per_device, mesh.shape["heads"]),
        mesh=mesh,
        in_specs=(P("views", "heads"), P("views", "heads"), P("views", "heads"), P()),
        out_specs=P(("views", "heads"), None),
        check_vma=False,
    )
```

```python
import functools

import jax
import jax.numpy as jnp
from jax import lax
from jax.experimental import pallas as pl
from jax.experimental.pallas import tpu as pltpu
from jax.sharding import PartitionSpec as P

HEAD_DIM = 64
SCALE = HEAD_DIM ** (-0.5) * 1.4426950408889634
X, Z = 4, 8
ONES = 16
PART = 512
FEW = 128
WIDE = 128
OWN = 16
SENT = 10
LIMIT = 2.0**100
VMEM = 48 * 2**20


def _dot(a, b, ca, cb):
    return lax.dot_general(a, b, (((ca,), (cb,)), ((), ())), preferred_element_type=jnp.float32)


def _copies_kernel(q_ref, copies_ref):
    n = q_ref.shape[1]
    row = lax.broadcasted_iota(jnp.int32, (n, n), 0)
    to = lax.broadcasted_iota(jnp.int32, (n, n), 1)
    move = row // OWN * 8 + row % 8 + row % OWN // 8 * (n // 2) == to
    q = _dot(q_ref[...], jnp.where(move, 1.0, 0.0).astype(jnp.bfloat16), 1, 0).astype(jnp.bfloat16)
    for z in range(copies_ref.shape[0]):
        copies_ref[z] = q


def _copies(q):
    return pl.pallas_call(
        _copies_kernel,
        out_shape=jax.ShapeDtypeStruct((Z, *q.shape), q.dtype),
        in_specs=[pl.BlockSpec(memory_space=pltpu.VMEM)],
        out_specs=pl.BlockSpec(memory_space=pltpu.VMEM),
        compiler_params=pltpu.CompilerParams(vmem_limit_bytes=8 * 2**20),
    )(q)


def _attend_kernel(chunks, first, last, *refs):
    q_ref, kv_refs = refs[0], refs[1 : 1 + chunks]
    state_ref = None if first else refs[1 + chunks]
    if last:
        out_ref, hold_ref, pack_ref = refs[-3:]
    else:
        out_ref = hold_ref = refs[-1]
    blocks, _, block = q_ref.shape
    rows = blocks * block
    keys = kv_refs[0].shape[1]
    scale = SCALE
    ones = jnp.ones((ONES, PART), jnp.bfloat16)

    def queries():
        parts = [q_ref[b, :, u * block // 2 : (u + 1) * block // 2] for u in range(2) for b in range(blocks)]
        return jnp.concatenate(parts, axis=1)

    def shifted(q, peak):
        at = lax.broadcasted_iota(jnp.int32, (ONES, rows), 0)
        return jnp.concatenate([q, jnp.where(at == 0, -peak, 0.0).astype(jnp.bfloat16)], axis=0)

    def highest(s):
        return jnp.max(s, axis=0, keepdims=True).astype(jnp.bfloat16).astype(jnp.float32)

    def score(kv_ref, at, q):
        return _dot(kv_ref[0:HEAD_DIM, pl.ds(at, PART)], q, 0, 0)

    def shifted_score(kv_ref, at, q):
        return _dot(jnp.concatenate([kv_ref[0:HEAD_DIM, pl.ds(at, PART)], ones], axis=0), q, 0, 0)

    def weigh(kv_ref, at, weights):
        v = jnp.concatenate([kv_ref[HEAD_DIM : 2 * HEAD_DIM, pl.ds(at, PART)], ones], axis=0)
        return _dot(v, weights.astype(jnp.bfloat16), 1, 0)

    total = None if first else state_ref[...]
    q = queries()
    peak = highest(_dot(kv_refs[0][0:HEAD_DIM, 0:FEW], q, 0, 0)) if first else state_ref[72:73, :]
    q = shifted(q, peak)
    for kv_ref in kv_refs:
        for at in range(0, keys, PART):
            more = weigh(kv_ref, at, jnp.exp2(shifted_score(kv_ref, at, q) * scale))
            total = more if total is None else total + more
    hold_ref[0:72, :] = total[0:72]
    hold_ref[72:80, :] = jnp.broadcast_to(peak, (8, rows))
    in_range = jnp.max(total[64:65]) < LIMIT

    @pl.when(jnp.logical_not(in_range))
    def _():
        q = queries()
        if first:
            hold_ref[0:72, :] = jnp.zeros((72, rows), jnp.float32)
            hold_ref[72:80, :] = jnp.full((8, rows), -1e30, jnp.float32)
        else:
            hold_ref[...] = state_ref[...]
        for kv_ref in kv_refs:

            @pl.loop(0, keys // PART)
            def _(i):
                at = pl.multiple_of(i * PART, PART)
                s = score(kv_ref, at, q)
                old = hold_ref[72:73, :]
                new = jnp.maximum(old, highest(s))
                more = weigh(kv_ref, at, jnp.exp2((s - new) * scale))
                hold_ref[0:72, :] = hold_ref[0:72, :] * jnp.exp2((old - new) * scale) + more[0:72]
                hold_ref[72:80, :] = jnp.broadcast_to(new, (8, rows))

    if last:
        def head(x):
            return x.astype(jnp.bfloat16).astype(jnp.float32)

        half = rows // 2
        count = half // 8
        both = jnp.concatenate([hold_ref[0:HEAD_DIM, :half], hold_ref[0:HEAD_DIM, half:]], axis=0).T
        t = hold_ref[64:72, :]
        p = hold_ref[72:80, :]
        t0 = head(t)
        terms = (t0, t - t0, p)
        owner = lax.broadcasted_iota(jnp.int32, (8, WIDE), 0)
        lane = lax.broadcasted_iota(jnp.int32, (8, WIDE), 1)
        mine = []
        for c in range(0, count, 8):
            at = c * 8 // WIDE * WIDE
            here = lane // 8 == owner + c % (WIDE // 8)
            cols = [jnp.where(here, x[:, u * half + at : u * half + at + WIDE], 0.0) for x in terms for u in range(2)]
            mine.append(jnp.concatenate(cols, axis=1).astype(jnp.bfloat16))
        source = lax.broadcasted_iota(jnp.int32, (6 * WIDE, WIDE), 0)
        to = lax.broadcasted_iota(jnp.int32, (6 * WIDE, WIDE), 1)
        move = jnp.where(source // WIDE * 8 + source % 8 == to, 1.0, 0.0).astype(jnp.bfloat16)
        tail = _dot(jnp.concatenate(mine, axis=0), move, 1, 0)
        for c in range(count):
            pack_ref[c * SENT : c * SENT + 8, :] = both[c * 8 : c * 8 + 8]
            pack_ref[c * SENT + 8 : c * SENT + 10, :] = jnp.broadcast_to(tail[c : c + 1], (2, WIDE))
        out_ref[...] = pack_ref[...].astype(jnp.bfloat16)


def _attend(q_all, kvs, state, last):
    blocks, _, block = q_all.shape
    rows = blocks * block
    state_type = jax.ShapeDtypeStruct((80, rows), jnp.float32)
    operands = (q_all, *kvs) + (() if state is None else (state,))
    keys = len(kvs) * kvs[0].shape[1]
    return pl.pallas_call(
        functools.partial(_attend_kernel, len(kvs), state is None, last),
        out_shape=jax.ShapeDtypeStruct((rows // OWN * SENT, WIDE), jnp.bfloat16) if last else state_type,
        in_specs=[pl.BlockSpec(memory_space=pltpu.VMEM)] * len(operands),
        out_specs=pl.BlockSpec(memory_space=pltpu.VMEM),
        scratch_shapes=[pltpu.VMEM((80, rows), jnp.float32), pltpu.VMEM((rows // OWN * SENT, WIDE), jnp.float32)]
        if last
        else [],
        compiler_params=pltpu.CompilerParams(vmem_limit_bytes=VMEM),
        cost_estimate=pl.CostEstimate(
            flops=4 * rows * keys * 256, bytes_accessed=2**21, transcendentals=rows * keys
        ),
    )(*operands)


def _finish_kernel(heads, got_ref, weight_ref, out_ref, pack_ref):
    senders = got_ref.shape[0] // (heads * SENT)
    pack_ref[...] = got_ref[...].astype(jnp.float32)
    lane = lax.broadcasted_iota(jnp.int32, (8, WIDE), 1)
    sub = lax.broadcasted_iota(jnp.int32, (8, WIDE), 0)
    mine = (lane % 8 == sub) & (lane < 3 * OWN)
    term = lax.broadcasted_iota(jnp.int32, (WIDE, 2 * WIDE), 0)
    to = lax.broadcasted_iota(jnp.int32, (WIDE, 2 * WIDE), 1)
    pick = ((term // OWN < 2) == (to < WIDE)) & ((term % OWN < 8) == (to % WIDE < HEAD_DIM))
    pick = jnp.where(pick, 1.0, 0.0).astype(jnp.bfloat16)
    parts, spread = [], []
    for s in range(senders):
        at = [(s * heads + h) * SENT for h in range(heads)]
        parts.append(jnp.concatenate([pack_ref[i : i + 8, :] for i in at], axis=0))
        tails = [jnp.where(mine, jnp.broadcast_to(pack_ref[i + 8 : i + 9, :], (8, WIDE)), 0.0) for i in at]
        spread.append(_dot(jnp.concatenate(tails, axis=0).astype(jnp.bfloat16), pick, 1, 0))
    top = spread[0][:, WIDE:]
    for s in spread[1:]:
        top = jnp.maximum(top, s[:, WIDE:])
    summed = jnp.zeros((8 * heads, WIDE), jnp.float32)
    total = jnp.zeros((8 * heads, WIDE), jnp.float32)
    for part, s in zip(parts, spread):
        factor = jnp.exp2((s[:, WIDE:] - top) * SCALE)
        summed += factor * part
        total += factor * s[:, :WIDE]
    out = summed / total
    acc = jnp.zeros(out_ref.shape, jnp.float32)
    per = 4
    for g in range(heads // per):
        pairs = []
        for h in range(g * per, (g + 1) * per, 2):
            even = out[h * 8 : (h + 1) * 8]
            odd = out[(h + 1) * 8 : (h + 2) * 8]
            low = jnp.where(lane < HEAD_DIM, even, pltpu.roll(odd, HEAD_DIM, 1))
            high = jnp.where(lane < HEAD_DIM, pltpu.roll(even, HEAD_DIM, 1), odd)
            pairs.append(jnp.concatenate([low, high], axis=0).astype(jnp.bfloat16))
        w = weight_ref[g * per * HEAD_DIM : (g + 1) * per * HEAD_DIM, :]
        acc += _dot(jnp.concatenate(pairs, axis=1), w, 1, 0)
    out_ref[...] = acc.astype(jnp.bfloat16)


def _finish(got, out_weight, heads):
    return pl.pallas_call(
        functools.partial(_finish_kernel, heads),
        out_shape=jax.ShapeDtypeStruct((OWN, out_weight.shape[1]), jnp.bfloat16),
        in_specs=[pl.BlockSpec(memory_space=pltpu.VMEM)] * 2,
        out_specs=pl.BlockSpec(memory_space=pltpu.VMEM),
        scratch_shapes=[pltpu.VMEM(got.shape, jnp.float32)],
        compiler_params=pltpu.CompilerParams(vmem_limit_bytes=VMEM),
    )(got, out_weight)


def per_device(heads, queries, keys, values, out_weight):
    z_groups = [[x * Z + z for z in range(Z)] for x in range(X)]
    zh_groups = [[(x * Z + z) * heads + h for z in range(Z) for h in range(heads)] for x in range(X)]

    def from_x(array, step):
        return lax.ppermute(
            array, "views", [(x * Z + z, (x + step) % X * Z + z) for x in range(X) for z in range(Z)]
        )

    kv = jnp.concatenate([keys.T, values.T], axis=0)
    kv2 = from_x(kv, 2)
    q_all = lax.all_to_all(_copies(queries.T), "views", 0, 0, tiled=True, axis_index_groups=z_groups)
    kv1, kv3 = from_x(kv, 1), from_x(kv, 3)
    state = _attend(q_all, (kv, kv2), None, False)
    state = _attend(q_all, (kv1,), state, False)
    rows = _attend(q_all, (kv3,), state, True)

    sent = rows.reshape(Z * heads * SENT // 2, 2, WIDE)
    got = lax.all_to_all(sent, ("views", "heads"), 0, 0, tiled=True, axis_index_groups=zh_groups)
    return _finish(got.reshape(Z * heads * SENT, WIDE), out_weight, heads)


def solution(mesh):
    assert mesh.shape["views"] == X * Z
    return jax.shard_map(
        functools.partial(per_device, mesh.shape["heads"]),
        mesh=mesh,
        in_specs=(P("views", "heads"), P("views", "heads"), P("views", "heads"), P()),
        out_specs=P(("views", "heads"), None),
        check_vma=False,
    )
```

```python
import functools

import jax
import jax.numpy as jnp
from jax import lax
from jax.experimental import pallas as pl
from jax.experimental.pallas import tpu as pltpu
from jax.sharding import PartitionSpec as P

HEAD_DIM = 64
SCALE = HEAD_DIM ** (-0.5) * 1.4426950408889634
X, Z = 4, 8
ONES = 16
PART = 512
FEW = 128
WIDE = 128
OWN = 16
SENT = 10
LIMIT = 2.0**100
VMEM = 48 * 2**20


def _dot(a, b, ca, cb):
    return lax.dot_general(a, b, (((ca,), (cb,)), ((), ())), preferred_element_type=jnp.float32)


def _copies_kernel(q_ref, copies_ref):
    n = q_ref.shape[1]
    row = lax.broadcasted_iota(jnp.int32, (n, n), 0)
    to = lax.broadcasted_iota(jnp.int32, (n, n), 1)
    move = row // OWN * 8 + row % 8 + row % OWN // 8 * (n // 2) == to
    q = _dot(q_ref[...], jnp.where(move, 1.0, 0.0).astype(jnp.bfloat16), 1, 0).astype(jnp.bfloat16)
    for z in range(copies_ref.shape[0]):
        copies_ref[z] = q


def _copies(q):
    return pl.pallas_call(
        _copies_kernel,
        out_shape=jax.ShapeDtypeStruct((Z, *q.shape), q.dtype),
        in_specs=[pl.BlockSpec(memory_space=pltpu.VMEM)],
        out_specs=pl.BlockSpec(memory_space=pltpu.VMEM),
        compiler_params=pltpu.CompilerParams(vmem_limit_bytes=8 * 2**20),
    )(q)


def _attend_kernel(chunks, first, last, *refs):
    q_ref, kv_refs = refs[0], refs[1 : 1 + chunks]
    state_ref = None if first else refs[1 + chunks]
    if last:
        out_ref, hold_ref, pack_ref = refs[-3:]
    else:
        out_ref = hold_ref = refs[-1]
    blocks, _, block = q_ref.shape
    rows = blocks * block
    keys = kv_refs[0].shape[1]
    scale = SCALE
    ones = jnp.ones((ONES, PART), jnp.bfloat16)

    def queries():
        parts = [q_ref[b, :, u * block // 2 : (u + 1) * block // 2] for u in range(2) for b in range(blocks)]
        return jnp.concatenate(parts, axis=1)

    def shifted(q, peak):
        at = lax.broadcasted_iota(jnp.int32, (ONES, rows), 0)
        return jnp.concatenate([q, jnp.where(at == 0, -peak, 0.0).astype(jnp.bfloat16)], axis=0)

    def highest(s):
        return jnp.max(s, axis=0, keepdims=True).astype(jnp.bfloat16).astype(jnp.float32)

    def score(kv_ref, at, q):
        return _dot(kv_ref[0:HEAD_DIM, pl.ds(at, PART)], q, 0, 0)

    def shifted_score(kv_ref, at, q):
        return _dot(jnp.concatenate([kv_ref[0:HEAD_DIM, pl.ds(at, PART)], ones], axis=0), q, 0, 0)

    def weigh(kv_ref, at, weights):
        v = jnp.concatenate([kv_ref[HEAD_DIM : 2 * HEAD_DIM, pl.ds(at, PART)], ones], axis=0)
        return _dot(v, weights.astype(jnp.bfloat16), 1, 0)

    total = None if first else state_ref[...]
    q = queries()
    peak = highest(_dot(kv_refs[0][0:HEAD_DIM, 0:FEW], q, 0, 0)) if first else state_ref[72:73, :]
    q = shifted(q, peak)
    for kv_ref in kv_refs:
        for at in range(0, keys, PART):
            more = weigh(kv_ref, at, jnp.exp2(shifted_score(kv_ref, at, q) * scale))
            total = more if total is None else total + more
    hold_ref[0:72, :] = total[0:72]
    hold_ref[72:80, :] = jnp.broadcast_to(peak, (8, rows))
    in_range = jnp.max(total[64:65]) < LIMIT

    @pl.when(jnp.logical_not(in_range))
    def _():
        q = queries()
        if first:
            hold_ref[0:72, :] = jnp.zeros((72, rows), jnp.float32)
            hold_ref[72:80, :] = jnp.full((8, rows), -1e30, jnp.float32)
        else:
            hold_ref[...] = state_ref[...]
        for kv_ref in kv_refs:

            @pl.loop(0, keys // PART)
            def _(i):
                at = pl.multiple_of(i * PART, PART)
                s = score(kv_ref, at, q)
                old = hold_ref[72:73, :]
                new = jnp.maximum(old, highest(s))
                more = weigh(kv_ref, at, jnp.exp2((s - new) * scale))
                hold_ref[0:72, :] = hold_ref[0:72, :] * jnp.exp2((old - new) * scale) + more[0:72]
                hold_ref[72:80, :] = jnp.broadcast_to(new, (8, rows))

    if last:
        def head(x):
            return x.astype(jnp.bfloat16).astype(jnp.float32)

        half = rows // 2
        count = half // 8
        both = jnp.concatenate([hold_ref[0:HEAD_DIM, :half], hold_ref[0:HEAD_DIM, half:]], axis=0).T
        t = hold_ref[64:72, :]
        p = hold_ref[72:80, :]
        t0 = head(t)
        terms = (t0, t - t0, p)
        owner = lax.broadcasted_iota(jnp.int32, (8, WIDE), 0)
        lane = lax.broadcasted_iota(jnp.int32, (8, WIDE), 1)
        mine = []
        for c in range(0, count, 8):
            at = c * 8 // WIDE * WIDE
            here = lane // 8 == owner + c % (WIDE // 8)
            cols = [jnp.where(here, x[:, u * half + at : u * half + at + WIDE], 0.0) for x in terms for u in range(2)]
            mine.append(jnp.concatenate(cols, axis=1).astype(jnp.bfloat16))
        source = lax.broadcasted_iota(jnp.int32, (6 * WIDE, WIDE), 0)
        to = lax.broadcasted_iota(jnp.int32, (6 * WIDE, WIDE), 1)
        move = jnp.where(source // WIDE * 8 + source % 8 == to, 1.0, 0.0).astype(jnp.bfloat16)
        tail = _dot(jnp.concatenate(mine, axis=0), move, 1, 0)
        for c in range(count):
            pack_ref[c * SENT : c * SENT + 8, :] = both[c * 8 : c * 8 + 8]
            pack_ref[c * SENT + 8 : c * SENT + 10, :] = jnp.broadcast_to(tail[c : c + 1], (2, WIDE))
        out_ref[...] = pack_ref[...].astype(jnp.bfloat16)


def _attend(q_all, kvs, state, last):
    blocks, _, block = q_all.shape
    rows = blocks * block
    state_type = jax.ShapeDtypeStruct((80, rows), jnp.float32)
    operands = (q_all, *kvs) + (() if state is None else (state,))
    keys = len(kvs) * kvs[0].shape[1]
    return pl.pallas_call(
        functools.partial(_attend_kernel, len(kvs), state is None, last),
        out_shape=jax.ShapeDtypeStruct((rows // OWN * SENT, WIDE), jnp.bfloat16) if last else state_type,
        in_specs=[pl.BlockSpec(memory_space=pltpu.VMEM)] * len(operands),
        out_specs=pl.BlockSpec(memory_space=pltpu.VMEM),
        scratch_shapes=[pltpu.VMEM((80, rows), jnp.float32), pltpu.VMEM((rows // OWN * SENT, WIDE), jnp.float32)]
        if last
        else [],
        compiler_params=pltpu.CompilerParams(vmem_limit_bytes=VMEM),
        cost_estimate=pl.CostEstimate(
            flops=4 * rows * keys * 256, bytes_accessed=2**21, transcendentals=rows * keys
        ),
    )(*operands)


def _finish_kernel(heads, got_ref, weight_ref, out_ref, pack_ref):
    senders = got_ref.shape[0] // (heads * SENT)
    pack_ref[...] = got_ref[...].astype(jnp.float32)
    lane = lax.broadcasted_iota(jnp.int32, (8, WIDE), 1)
    sub = lax.broadcasted_iota(jnp.int32, (8, WIDE), 0)
    mine = (lane % 8 == sub) & (lane < 3 * OWN)
    term = lax.broadcasted_iota(jnp.int32, (WIDE, 2 * WIDE), 0)
    to = lax.broadcasted_iota(jnp.int32, (WIDE, 2 * WIDE), 1)
    pick = ((term // OWN < 2) == (to < WIDE)) & ((term % OWN < 8) == (to % WIDE < HEAD_DIM))
    pick = jnp.where(pick, 1.0, 0.0).astype(jnp.bfloat16)
    parts, spread = [], []
    for s in range(senders):
        at = [(s * heads + h) * SENT for h in range(heads)]
        parts.append(jnp.concatenate([pack_ref[i : i + 8, :] for i in at], axis=0))
        tails = [jnp.where(mine, jnp.broadcast_to(pack_ref[i + 8 : i + 9, :], (8, WIDE)), 0.0) for i in at]
        spread.append(_dot(jnp.concatenate(tails, axis=0).astype(jnp.bfloat16), pick, 1, 0))
    top = spread[0][:, WIDE:]
    for s in spread[1:]:
        top = jnp.maximum(top, s[:, WIDE:])
    summed = jnp.zeros((8 * heads, WIDE), jnp.float32)
    total = jnp.zeros((8 * heads, WIDE), jnp.float32)
    for part, s in zip(parts, spread):
        factor = jnp.exp2((s[:, WIDE:] - top) * SCALE)
        summed += factor * part
        total += factor * s[:, :WIDE]
    out = summed / total
    acc = jnp.zeros(out_ref.shape, jnp.float32)
    per = 4
    for g in range(heads // per):
        pairs = []
        for h in range(g * per, (g + 1) * per, 2):
            even = out[h * 8 : (h + 1) * 8]
            odd = out[(h + 1) * 8 : (h + 2) * 8]
            low = jnp.where(lane < HEAD_DIM, even, pltpu.roll(odd, HEAD_DIM, 1))
            high = jnp.where(lane < HEAD_DIM, pltpu.roll(even, HEAD_DIM, 1), odd)
            pairs.append(jnp.concatenate([low, high], axis=0).astype(jnp.bfloat16))
        w = weight_ref[g * per * HEAD_DIM : (g + 1) * per * HEAD_DIM, :]
        acc += _dot(jnp.concatenate(pairs, axis=1), w, 1, 0)
    out_ref[...] = acc.astype(jnp.bfloat16)


def _finish(got, out_weight, heads):
    return pl.pallas_call(
        functools.partial(_finish_kernel, heads),
        out_shape=jax.ShapeDtypeStruct((OWN, out_weight.shape[1]), jnp.bfloat16),
        in_specs=[pl.BlockSpec(memory_space=pltpu.VMEM)] * 2,
        out_specs=pl.BlockSpec(memory_space=pltpu.VMEM),
        scratch_shapes=[pltpu.VMEM(got.shape, jnp.float32)],
        compiler_params=pltpu.CompilerParams(vmem_limit_bytes=VMEM),
    )(got, out_weight)


def per_device(heads, queries, keys, values, out_weight):
    z_groups = [[x * Z + z for z in range(Z)] for x in range(X)]
    zh_groups = [[(x * Z + z) * heads + h for z in range(Z) for h in range(heads)] for x in range(X)]

    def swap_x(array, bits):
        pairs = [(x * Z + z, (x ^ bits) * Z + z) for x in range(X) for z in range(Z)]
        return lax.ppermute(array, "views", pairs)

    kv = jnp.concatenate([keys.T, values.T], axis=0)
    kv2 = swap_x(kv, 2)
    q_all = lax.all_to_all(_copies(queries.T), "views", 0, 0, tiled=True, axis_index_groups=z_groups)
    kv1, kv3 = swap_x(kv, 1), swap_x(kv, 3)
    state = _attend(q_all, (kv, kv2), None, False)
    state = _attend(q_all, (kv1,), state, False)
    rows = _attend(q_all, (kv3,), state, True)

    sent = rows.reshape(Z * heads * SENT // 2, 2, WIDE)
    got = lax.all_to_all(sent, ("views", "heads"), 0, 0, tiled=True, axis_index_groups=zh_groups)
    return _finish(got.reshape(Z * heads * SENT, WIDE), out_weight, heads)


def solution(mesh):
    assert mesh.shape["views"] == X * Z
    return jax.shard_map(
        functools.partial(per_device, mesh.shape["heads"]),
        mesh=mesh,
        in_specs=(P("views", "heads"), P("views", "heads"), P("views", "heads"), P()),
        out_specs=P(("views", "heads"), None),
        check_vma=False,
    )
```

```python
import functools

import jax
import jax.numpy as jnp
from jax import lax
from jax.experimental import pallas as pl
from jax.experimental.pallas import tpu as pltpu
from jax.sharding import PartitionSpec as P

HEAD_DIM = 64
SCALE = HEAD_DIM ** (-0.5) * 1.4426950408889634
X, Z = 4, 8
ORDER = (0, 2, 4, 6, 7, 5, 3, 1)
ONES = 16
PART = 512
FEW = 64
WIDE = 128
OWN = 16
SENT = 10
LIMIT = 2.0**100
VMEM = 48 * 2**20


def _dot(a, b, ca, cb):
    return lax.dot_general(a, b, (((ca,), (cb,)), ((), ())), preferred_element_type=jnp.float32)


def _copies_kernel(q_ref, copies_ref):
    n = q_ref.shape[1]
    row = lax.broadcasted_iota(jnp.int32, (n, n), 0)
    to = lax.broadcasted_iota(jnp.int32, (n, n), 1)
    move = row // OWN * 8 + row % 8 + row % OWN // 8 * (n // 2) == to
    q = _dot(q_ref[...], jnp.where(move, 1.0, 0.0).astype(jnp.bfloat16), 1, 0).astype(jnp.bfloat16)
    for z in range(copies_ref.shape[0]):
        copies_ref[z] = q


def _copies(q):
    return pl.pallas_call(
        _copies_kernel,
        out_shape=jax.ShapeDtypeStruct((Z, *q.shape), q.dtype),
        in_specs=[pl.BlockSpec(memory_space=pltpu.VMEM)],
        out_specs=pl.BlockSpec(memory_space=pltpu.VMEM),
        compiler_params=pltpu.CompilerParams(vmem_limit_bytes=8 * 2**20),
    )(q)


def _attend_kernel(chunks, first, last, *refs):
    q_ref, kv_refs = refs[0], refs[1 : 1 + chunks]
    state_ref = None if first else refs[1 + chunks]
    if last:
        out_ref, hold_ref, pack_ref = refs[-3:]
    else:
        out_ref = hold_ref = refs[-1]
    blocks, _, block = q_ref.shape
    rows = blocks * block
    keys = kv_refs[0].shape[1]
    scale = SCALE
    ones = jnp.ones((ONES, PART), jnp.bfloat16)

    def queries():
        parts = [q_ref[b, :, u * block // 2 : (u + 1) * block // 2] for u in range(2) for b in range(blocks)]
        return jnp.concatenate(parts, axis=1)

    def shifted(q, peak):
        at = lax.broadcasted_iota(jnp.int32, (ONES, rows), 0)
        return jnp.concatenate([q, jnp.where(at == 0, -peak, 0.0).astype(jnp.bfloat16)], axis=0)

    def highest(s):
        return jnp.max(s, axis=0, keepdims=True).astype(jnp.bfloat16).astype(jnp.float32)

    def score(kv_ref, at, q):
        return _dot(kv_ref[0:HEAD_DIM, pl.ds(at, PART)], q, 0, 0)

    def shifted_score(kv_ref, at, q):
        return _dot(jnp.concatenate([kv_ref[0:HEAD_DIM, pl.ds(at, PART)], ones], axis=0), q, 0, 0)

    def weigh(kv_ref, at, weights):
        v = jnp.concatenate([kv_ref[HEAD_DIM : 2 * HEAD_DIM, pl.ds(at, PART)], ones], axis=0)
        return _dot(v, weights.astype(jnp.bfloat16), 1, 0)

    total = None if first else state_ref[...]
    q = queries()
    peak = highest(_dot(kv_refs[0][0:HEAD_DIM, 0:FEW], q, 0, 0)) if first else state_ref[72:73, :]
    q = shifted(q, peak)
    for kv_ref in kv_refs:
        for at in range(0, keys, PART):
            more = weigh(kv_ref, at, jnp.exp2(shifted_score(kv_ref, at, q) * scale))
            total = more if total is None else total + more
    hold_ref[0:72, :] = total[0:72]
    hold_ref[72:80, :] = jnp.broadcast_to(peak, (8, rows))
    in_range = jnp.max(total[64:65]) < LIMIT

    @pl.when(jnp.logical_not(in_range))
    def _():
        q = queries()
        if first:
            hold_ref[0:72, :] = jnp.zeros((72, rows), jnp.float32)
            hold_ref[72:80, :] = jnp.full((8, rows), -1e30, jnp.float32)
        else:
            hold_ref[...] = state_ref[...]
        for kv_ref in kv_refs:

            @pl.loop(0, keys // PART)
            def _(i):
                at = pl.multiple_of(i * PART, PART)
                s = score(kv_ref, at, q)
                old = hold_ref[72:73, :]
                new = jnp.maximum(old, highest(s))
                more = weigh(kv_ref, at, jnp.exp2((s - new) * scale))
                hold_ref[0:72, :] = hold_ref[0:72, :] * jnp.exp2((old - new) * scale) + more[0:72]
                hold_ref[72:80, :] = jnp.broadcast_to(new, (8, rows))

    if last:
        def head(x):
            return x.astype(jnp.bfloat16).astype(jnp.float32)

        half = rows // 2
        count = half // 8
        both = jnp.concatenate([hold_ref[0:HEAD_DIM, :half], hold_ref[0:HEAD_DIM, half:]], axis=0).T
        t = hold_ref[64:72, :]
        p = hold_ref[72:80, :]
        t0 = head(t)
        terms = (t0, t - t0, p)
        owner = lax.broadcasted_iota(jnp.int32, (8, WIDE), 0)
        lane = lax.broadcasted_iota(jnp.int32, (8, WIDE), 1)
        mine = []
        for c in range(0, count, 8):
            at = c * 8 // WIDE * WIDE
            here = lane // 8 == owner + c % (WIDE // 8)
            cols = [jnp.where(here, x[:, u * half + at : u * half + at + WIDE], 0.0) for x in terms for u in range(2)]
            mine.append(jnp.concatenate(cols, axis=1).astype(jnp.bfloat16))
        source = lax.broadcasted_iota(jnp.int32, (6 * WIDE, WIDE), 0)
        to = lax.broadcasted_iota(jnp.int32, (6 * WIDE, WIDE), 1)
        move = jnp.where(source // WIDE * 8 + source % 8 == to, 1.0, 0.0).astype(jnp.bfloat16)
        tail = _dot(jnp.concatenate(mine, axis=0), move, 1, 0)
        for c in range(count):
            pack_ref[c * SENT : c * SENT + 8, :] = both[c * 8 : c * 8 + 8]
            pack_ref[c * SENT + 8 : c * SENT + 10, :] = jnp.broadcast_to(tail[c : c + 1], (2, WIDE))
        out_ref[...] = pack_ref[...].astype(jnp.bfloat16)


def _attend(q_all, kvs, state, last):
    blocks, _, block = q_all.shape
    rows = blocks * block
    state_type = jax.ShapeDtypeStruct((80, rows), jnp.float32)
    operands = (q_all, *kvs) + (() if state is None else (state,))
    keys = len(kvs) * kvs[0].shape[1]
    return pl.pallas_call(
        functools.partial(_attend_kernel, len(kvs), state is None, last),
        out_shape=jax.ShapeDtypeStruct((rows // OWN * SENT, WIDE), jnp.bfloat16) if last else state_type,
        in_specs=[pl.BlockSpec(memory_space=pltpu.VMEM)] * len(operands),
        out_specs=pl.BlockSpec(memory_space=pltpu.VMEM),
        scratch_shapes=[pltpu.VMEM((80, rows), jnp.float32), pltpu.VMEM((rows // OWN * SENT, WIDE), jnp.float32)]
        if last
        else [],
        compiler_params=pltpu.CompilerParams(vmem_limit_bytes=VMEM),
        cost_estimate=pl.CostEstimate(
            flops=4 * rows * keys * 256, bytes_accessed=2**21, transcendentals=rows * keys
        ),
    )(*operands)


def _finish_kernel(heads, got_ref, weight_ref, out_ref, pack_ref):
    senders = got_ref.shape[0] // (heads * SENT)
    pack_ref[...] = got_ref[...].astype(jnp.float32)
    lane = lax.broadcasted_iota(jnp.int32, (8, WIDE), 1)
    sub = lax.broadcasted_iota(jnp.int32, (8, WIDE), 0)
    mine = (lane % 8 == sub) & (lane < 3 * OWN)
    term = lax.broadcasted_iota(jnp.int32, (WIDE, 2 * WIDE), 0)
    to = lax.broadcasted_iota(jnp.int32, (WIDE, 2 * WIDE), 1)
    pick = ((term // OWN < 2) == (to < WIDE)) & ((term % OWN < 8) == (to % WIDE < HEAD_DIM))
    pick = jnp.where(pick, 1.0, 0.0).astype(jnp.bfloat16)
    parts, spread = [], []
    for s in range(senders):
        at = [(s * heads + h) * SENT for h in range(heads)]
        parts.append(jnp.concatenate([pack_ref[i : i + 8, :] for i in at], axis=0))
        tails = [jnp.where(mine, jnp.broadcast_to(pack_ref[i + 8 : i + 9, :], (8, WIDE)), 0.0) for i in at]
        spread.append(_dot(jnp.concatenate(tails, axis=0).astype(jnp.bfloat16), pick, 1, 0))
    top = spread[0][:, WIDE:]
    for s in spread[1:]:
        top = jnp.maximum(top, s[:, WIDE:])
    summed = jnp.zeros((8 * heads, WIDE), jnp.float32)
    total = jnp.zeros((8 * heads, WIDE), jnp.float32)
    for part, s in zip(parts, spread):
        factor = jnp.exp2((s[:, WIDE:] - top) * SCALE)
        summed += factor * part
        total += factor * s[:, :WIDE]
    out = summed / total
    acc = jnp.zeros(out_ref.shape, jnp.float32)
    per = 4
    for g in range(heads // per):
        pairs = []
        for h in range(g * per, (g + 1) * per, 2):
            even = out[h * 8 : (h + 1) * 8]
            odd = out[(h + 1) * 8 : (h + 2) * 8]
            low = jnp.where(lane < HEAD_DIM, even, pltpu.roll(odd, HEAD_DIM, 1))
            high = jnp.where(lane < HEAD_DIM, pltpu.roll(even, HEAD_DIM, 1), odd)
            pairs.append(jnp.concatenate([low, high], axis=0).astype(jnp.bfloat16))
        w = weight_ref[g * per * HEAD_DIM : (g + 1) * per * HEAD_DIM, :]
        acc += _dot(jnp.concatenate(pairs, axis=1), w, 1, 0)
    out_ref[...] = acc.astype(jnp.bfloat16)


def _finish(got, out_weight, heads):
    return pl.pallas_call(
        functools.partial(_finish_kernel, heads),
        out_shape=jax.ShapeDtypeStruct((OWN, out_weight.shape[1]), jnp.bfloat16),
        in_specs=[pl.BlockSpec(memory_space=pltpu.VMEM)] * 2,
        out_specs=pl.BlockSpec(memory_space=pltpu.VMEM),
        scratch_shapes=[pltpu.VMEM(got.shape, jnp.float32)],
        compiler_params=pltpu.CompilerParams(vmem_limit_bytes=VMEM),
    )(got, out_weight)


def per_device(heads, queries, keys, values, out_weight):
    z_groups = [[x * Z + z for z in ORDER] for x in range(X)]
    zh_groups = [[(x * Z + z) * heads + h for z in ORDER for h in range(heads)] for x in range(X)]

    def swap_x(array, bits):
        pairs = [(x * Z + z, (x ^ bits) * Z + z) for x in range(X) for z in range(Z)]
        return lax.ppermute(array, "views", pairs)

    kv = jnp.concatenate([keys.T, values.T], axis=0)
    kv2 = swap_x(kv, 2)
    q_all = lax.all_to_all(_copies(queries.T), "views", 0, 0, tiled=True, axis_index_groups=z_groups)
    kv1, kv3 = swap_x(kv, 1), swap_x(kv, 3)
    state = _attend(q_all, (kv, kv2), None, False)
    state = _attend(q_all, (kv1,), state, False)
    rows = _attend(q_all, (kv3,), state, True)

    sent = rows.reshape(Z * heads * SENT // 2, 2, WIDE)
    got = lax.all_to_all(sent, ("views", "heads"), 0, 0, tiled=True, axis_index_groups=zh_groups)
    return _finish(got.reshape(Z * heads * SENT, WIDE), out_weight, heads)


def solution(mesh):
    assert mesh.shape["views"] == X * Z
    return jax.shard_map(
        functools.partial(per_device, mesh.shape["heads"]),
        mesh=mesh,
        in_specs=(P("views", "heads"), P("views", "heads"), P("views", "heads"), P()),
        out_specs=P(("views", "heads"), None),
        check_vma=False,
    )
```

```python
import functools

import jax
import jax.numpy as jnp
from jax import lax
from jax.experimental import pallas as pl
from jax.experimental.pallas import tpu as pltpu
from jax.sharding import PartitionSpec as P

HEAD_DIM = 64
SCALE = HEAD_DIM ** (-0.5) * 1.4426950408889634
X, Z = 4, 8
ORDER = (0, 2, 4, 6, 7, 5, 3, 1)
ONES = 16
PART = 512
FEW = 64
WIDE = 128
OWN = 16
SENT = 10
LIMIT = 2.0**100
VMEM = 48 * 2**20


def _dot(a, b, ca, cb):
    return lax.dot_general(a, b, (((ca,), (cb,)), ((), ())), preferred_element_type=jnp.float32)


def _copies_kernel(q_ref, copies_ref):
    n = q_ref.shape[1]
    row = lax.broadcasted_iota(jnp.int32, (n, n), 0)
    to = lax.broadcasted_iota(jnp.int32, (n, n), 1)
    move = row // OWN * 8 + row % 8 + row % OWN // 8 * (n // 2) == to
    q = _dot(q_ref[...], jnp.where(move, 1.0, 0.0).astype(jnp.bfloat16), 1, 0).astype(jnp.bfloat16)
    for z in range(copies_ref.shape[0]):
        copies_ref[z] = q


def _copies(q):
    return pl.pallas_call(
        _copies_kernel,
        out_shape=jax.ShapeDtypeStruct((Z, *q.shape), q.dtype),
        in_specs=[pl.BlockSpec(memory_space=pltpu.VMEM)],
        out_specs=pl.BlockSpec(memory_space=pltpu.VMEM),
        compiler_params=pltpu.CompilerParams(vmem_limit_bytes=8 * 2**20),
    )(q)


def _attend_kernel(chunks, seen, last, *refs):
    q_ref, kv_refs, seen_refs = refs[0], refs[1 : 1 + chunks], refs[1 + chunks : 1 + chunks + seen]
    first = not last and len(refs) == 2 + chunks
    state_ref = None if first else refs[1 + chunks + seen]
    if last:
        out_ref, hold_ref, pack_ref = refs[-3:]
    else:
        out_ref = hold_ref = refs[-1]
    blocks, _, block = q_ref.shape
    rows = blocks * block
    keys = kv_refs[0].shape[1]
    scale = SCALE
    ones = jnp.ones((ONES, PART), jnp.bfloat16)

    def queries():
        parts = [q_ref[b, :, u * block // 2 : (u + 1) * block // 2] for u in range(2) for b in range(blocks)]
        return jnp.concatenate(parts, axis=1)

    def shifted(q, peak):
        at = lax.broadcasted_iota(jnp.int32, (ONES, rows), 0)
        return jnp.concatenate([q, jnp.where(at == 0, -peak, 0.0).astype(jnp.bfloat16)], axis=0)

    def highest(s):
        return jnp.max(s, axis=0, keepdims=True).astype(jnp.bfloat16).astype(jnp.float32)

    def score(kv_ref, at, q):
        return _dot(kv_ref[0:HEAD_DIM, pl.ds(at, PART)], q, 0, 0)

    def shifted_score(kv_ref, at, q):
        return _dot(jnp.concatenate([kv_ref[0:HEAD_DIM, pl.ds(at, PART)], ones], axis=0), q, 0, 0)

    def weigh(kv_ref, at, weights):
        v = jnp.concatenate([kv_ref[HEAD_DIM : 2 * HEAD_DIM, pl.ds(at, PART)], ones], axis=0)
        return _dot(v, weights.astype(jnp.bfloat16), 1, 0)

    total = None if first else state_ref[...]
    q = queries()
    peak = highest(_dot(kv_refs[0][0:HEAD_DIM, 0:FEW], q, 0, 0)) if first else state_ref[72:73, :]
    q = shifted(q, peak)
    for kv_ref in kv_refs:
        for at in range(0, keys, PART):
            more = weigh(kv_ref, at, jnp.exp2(shifted_score(kv_ref, at, q) * scale))
            total = more if total is None else total + more
    hold_ref[0:72, :] = total[0:72]
    hold_ref[72:80, :] = jnp.broadcast_to(peak, (8, rows))
    if not last:
        return
    in_range = jnp.max(total[64:65]) < LIMIT

    @pl.when(jnp.logical_not(in_range))
    def _():
        q = queries()
        hold_ref[0:72, :] = jnp.zeros((72, rows), jnp.float32)
        hold_ref[72:80, :] = jnp.full((8, rows), -1e30, jnp.float32)
        for kv_ref in (*seen_refs, *kv_refs):

            @pl.loop(0, keys // PART)
            def _(i):
                at = pl.multiple_of(i * PART, PART)
                s = score(kv_ref, at, q)
                old = hold_ref[72:73, :]
                new = jnp.maximum(old, highest(s))
                more = weigh(kv_ref, at, jnp.exp2((s - new) * scale))
                hold_ref[0:72, :] = hold_ref[0:72, :] * jnp.exp2((old - new) * scale) + more[0:72]
                hold_ref[72:80, :] = jnp.broadcast_to(new, (8, rows))

    if last:
        def head(x):
            return x.astype(jnp.bfloat16).astype(jnp.float32)

        half = rows // 2
        count = half // 8
        both = jnp.concatenate([hold_ref[0:HEAD_DIM, :half], hold_ref[0:HEAD_DIM, half:]], axis=0).T
        t = hold_ref[64:72, :]
        p = hold_ref[72:80, :]
        t0 = head(t)
        terms = (t0, t - t0, p)
        owner = lax.broadcasted_iota(jnp.int32, (8, WIDE), 0)
        lane = lax.broadcasted_iota(jnp.int32, (8, WIDE), 1)
        mine = []
        for c in range(0, count, 8):
            at = c * 8 // WIDE * WIDE
            here = lane // 8 == owner + c % (WIDE // 8)
            cols = [jnp.where(here, x[:, u * half + at : u * half + at + WIDE], 0.0) for x in terms for u in range(2)]
            mine.append(jnp.concatenate(cols, axis=1).astype(jnp.bfloat16))
        source = lax.broadcasted_iota(jnp.int32, (6 * WIDE, WIDE), 0)
        to = lax.broadcasted_iota(jnp.int32, (6 * WIDE, WIDE), 1)
        move = jnp.where(source // WIDE * 8 + source % 8 == to, 1.0, 0.0).astype(jnp.bfloat16)
        tail = _dot(jnp.concatenate(mine, axis=0), move, 1, 0)
        for c in range(count):
            pack_ref[c * SENT : c * SENT + 8, :] = both[c * 8 : c * 8 + 8]
            pack_ref[c * SENT + 8 : c * SENT + 10, :] = jnp.broadcast_to(tail[c : c + 1], (2, WIDE))
        out_ref[...] = pack_ref[...].astype(jnp.bfloat16)


def _attend(q_all, kvs, state, seen=(), last=False):
    blocks, _, block = q_all.shape
    rows = blocks * block
    state_type = jax.ShapeDtypeStruct((80, rows), jnp.float32)
    operands = (q_all, *kvs, *seen) + (() if state is None else (state,))
    keys = len(kvs) * kvs[0].shape[1]
    return pl.pallas_call(
        functools.partial(_attend_kernel, len(kvs), len(seen), last),
        out_shape=jax.ShapeDtypeStruct((rows // OWN * SENT, WIDE), jnp.bfloat16) if last else state_type,
        in_specs=[pl.BlockSpec(memory_space=pltpu.VMEM)] * len(operands),
        out_specs=pl.BlockSpec(memory_space=pltpu.VMEM),
        scratch_shapes=[pltpu.VMEM((80, rows), jnp.float32), pltpu.VMEM((rows // OWN * SENT, WIDE), jnp.float32)]
        if last
        else [],
        compiler_params=pltpu.CompilerParams(vmem_limit_bytes=VMEM),
        cost_estimate=pl.CostEstimate(
            flops=4 * rows * keys * 256, bytes_accessed=2**21, transcendentals=rows * keys
        ),
    )(*operands)


def _finish_kernel(heads, got_ref, weight_ref, out_ref, pack_ref):
    senders = got_ref.shape[0] // (heads * SENT)
    pack_ref[...] = got_ref[...].astype(jnp.float32)
    lane = lax.broadcasted_iota(jnp.int32, (8, WIDE), 1)
    sub = lax.broadcasted_iota(jnp.int32, (8, WIDE), 0)
    mine = (lane % 8 == sub) & (lane < 3 * OWN)
    term = lax.broadcasted_iota(jnp.int32, (WIDE, 2 * WIDE), 0)
    to = lax.broadcasted_iota(jnp.int32, (WIDE, 2 * WIDE), 1)
    pick = ((term // OWN < 2) == (to < WIDE)) & ((term % OWN < 8) == (to % WIDE < HEAD_DIM))
    pick = jnp.where(pick, 1.0, 0.0).astype(jnp.bfloat16)
    parts, spread = [], []
    for s in range(senders):
        at = [(s * heads + h) * SENT for h in range(heads)]
        parts.append(jnp.concatenate([pack_ref[i : i + 8, :] for i in at], axis=0))
        tails = [jnp.where(mine, jnp.broadcast_to(pack_ref[i + 8 : i + 9, :], (8, WIDE)), 0.0) for i in at]
        spread.append(_dot(jnp.concatenate(tails, axis=0).astype(jnp.bfloat16), pick, 1, 0))
    top = spread[0][:, WIDE:]
    for s in spread[1:]:
        top = jnp.maximum(top, s[:, WIDE:])
    summed = jnp.zeros((8 * heads, WIDE), jnp.float32)
    total = jnp.zeros((8 * heads, WIDE), jnp.float32)
    for part, s in zip(parts, spread):
        factor = jnp.exp2((s[:, WIDE:] - top) * SCALE)
        summed += factor * part
        total += factor * s[:, :WIDE]
    out = summed / total
    acc = jnp.zeros(out_ref.shape, jnp.float32)
    per = 4
    for g in range(heads // per):
        pairs = []
        for h in range(g * per, (g + 1) * per, 2):
            even = out[h * 8 : (h + 1) * 8]
            odd = out[(h + 1) * 8 : (h + 2) * 8]
            low = jnp.where(lane < HEAD_DIM, even, pltpu.roll(odd, HEAD_DIM, 1))
            high = jnp.where(lane < HEAD_DIM, pltpu.roll(even, HEAD_DIM, 1), odd)
            pairs.append(jnp.concatenate([low, high], axis=0).astype(jnp.bfloat16))
        w = weight_ref[g * per * HEAD_DIM : (g + 1) * per * HEAD_DIM, :]
        acc += _dot(jnp.concatenate(pairs, axis=1), w, 1, 0)
    out_ref[...] = acc.astype(jnp.bfloat16)


def _finish(got, out_weight, heads):
    return pl.pallas_call(
        functools.partial(_finish_kernel, heads),
        out_shape=jax.ShapeDtypeStruct((OWN, out_weight.shape[1]), jnp.bfloat16),
        in_specs=[pl.BlockSpec(memory_space=pltpu.VMEM)] * 2,
        out_specs=pl.BlockSpec(memory_space=pltpu.VMEM),
        scratch_shapes=[pltpu.VMEM(got.shape, jnp.float32)],
        compiler_params=pltpu.CompilerParams(vmem_limit_bytes=VMEM),
    )(got, out_weight)


def per_device(heads, queries, keys, values, out_weight):
    z_groups = [[x * Z + z for z in ORDER] for x in range(X)]
    zh_groups = [[(x * Z + z) * heads + h for z in ORDER for h in range(heads)] for x in range(X)]

    def swap_x(array, bits):
        pairs = [(x * Z + z, (x ^ bits) * Z + z) for x in range(X) for z in range(Z)]
        return lax.ppermute(array, "views", pairs)

    kv = jnp.concatenate([keys.T, values.T], axis=0)
    kv2 = swap_x(kv, 2)
    q_all = lax.all_to_all(_copies(queries.T), "views", 0, 0, tiled=True, axis_index_groups=z_groups)
    kv1, kv3 = swap_x(kv, 1), swap_x(kv, 3)
    state = _attend(q_all, (kv, kv2), None)
    state = _attend(q_all, (kv1,), state)
    rows = _attend(q_all, (kv3,), state, (kv, kv2, kv1), True)

    sent = rows.reshape(Z * heads * SENT // 2, 2, WIDE)
    got = lax.all_to_all(sent, ("views", "heads"), 0, 0, tiled=True, axis_index_groups=zh_groups)
    return _finish(got.reshape(Z * heads * SENT, WIDE), out_weight, heads)


def solution(mesh):
    assert mesh.shape["views"] == X * Z
    return jax.shard_map(
        functools.partial(per_device, mesh.shape["heads"]),
        mesh=mesh,
        in_specs=(P("views", "heads"), P("views", "heads"), P("views", "heads"), P()),
        out_specs=P(("views", "heads"), None),
        check_vma=False,
    )
```
